256 devices in a mesh: wall: 8 (over y, core), span: 4 (over x), stream: 8 (over z).
Axes of the slice: x: 4, y: 4, z: 8, core: 2. Of those that a mesh axis runs over, the one named last changes fastest.
Arguments:
- velocity: float32 [3, 1536, 128, 512], P(None, 'wall', 'stream', 'span'), may hold values from -6 to 6
- viscosity: float32 [1536], replicated, may hold values from 82944 to 165888
Outputs:
- predictor: float32 [3, 1536, 128, 512], P(None, 'wall', 'stream', 'span')
- velocity_new: float32 [3, 1536, 128, 512], P(None, 'wall', 'stream', 'span')
The draws below stay inside these ranges and needn't reach their ends.
All inputs are finite; a program needn't handle non-finite values.
Results may differ from the reference program's by a relative error of at most 0.00055.
Values sent between devices are 32-bit elements; how exact they have to be, the bound alone decides.
No kernel may reach another device: no remote copies, remote signals or barrier semaphores. Data moves between devices by JAX's collectives and lax.ppermute only.
A program may use at most 192 MiB of HBM per device.

```python
import math
import jax
import jax.numpy as jnp
from jax import lax

NY = 1536
NX = 128
NZ = 512


def levels(stream_key, shape, shards, least, top_value):
    level, own = 1.0, jax.random.fold_in(stream_key, 6)
    for dim, parts in shards:
        heights = jnp.exp(jax.random.uniform(jax.random.fold_in(own, dim), (parts,), jnp.float32, least / len(shards), top_value / len(shards)))
        level = level * jnp.repeat(heights, shape[dim] // parts).reshape([-1 if axis == dim else 1 for axis in range(len(shape))])
    return level


def scatter_about(rng, extent, width, bound, cuts=(), kind=jnp.bfloat16):
    entries = jax.random.normal(rng, extent, jnp.float32) * width
    if len(cuts) > 0:
        entries = levels(rng, extent, cuts, -0.22, 0.18) * entries
    return jnp.clip(entries, min=-bound, max=bound).astype(kind)


def setup_inputs(seed: int = 0) -> dict:
    key_of = jax.random.split(jax.random.key(seed), 3)
    velocity = scatter_about(key_of[0], (3, NY, NX, NZ), 1.0, 6.0, ((1, 8), (2, 8), (3, 4)), jnp.float32)
    viscosity = jnp.clip(jnp.exp(jax.random.uniform(key_of[1], (NY,), jnp.float32, math.log(82944.0), math.log(165888.0))), 82944.0, 165888.0)
    return {"velocity": velocity, "viscosity": viscosity}


step_size = 0.5


def sixth_order_stencil(field, along_axis):
    def moved(offset):
        return jnp.roll(field, -offset, axis=along_axis)
    return (45.0 * (moved(1) - moved(-1)) - 9.0 * (moved(2) - moved(-2)) + (moved(3) - moved(-3))) / 60.0


def wall_slope(field):
    padded = jnp.pad(field, ((1, 1), (0, 0), (0, 0)))
    return (padded[2:] - padded[:-2]) * 0.5


def line_solve(field, lower_coef, center_coef, upper_coefficient):
    tail_shape = field.shape[1:]

    def forward(state_now, inputs):
        prime_prev, value_prev = state_now
        lower_now, center_now, upper_now, rhs_now = inputs
        pivot_value = center_now - lower_now * prime_prev
        prime_next = upper_now / pivot_value
        value_next = (rhs_now - lower_now * value_prev) / pivot_value
        return (prime_next, value_next), (prime_next, value_next)

    initial = (jnp.zeros((), jnp.float32), jnp.zeros(tail_shape, jnp.float32))
    closing_state, outputs = lax.scan(forward, initial, (lower_coef, center_coef, upper_coefficient, field))

    def backward(later_value, inputs):
        prime_now, value_now = inputs
        solved = value_now - prime_now * later_value
        return solved, solved

    final_value, solved_all = lax.scan(backward, jnp.zeros(tail_shape, jnp.float32), outputs, reverse=True)
    return solved_all


def reference(velocity, viscosity):
    length = viscosity.shape[0]
    face_high = jnp.concatenate([viscosity[1:], viscosity[-1:]])
    center_coef = 1.0 + viscosity + face_high
    positions = jnp.arange(length)
    lower_coef = jnp.where(positions > 0, -viscosity, jnp.zeros_like(viscosity))
    upper_coefficient = jnp.where(positions < length - 1, -face_high, jnp.zeros_like(face_high))
    predicted = []
    solutions = []
    for component in range(3):
        field = velocity[component]
        advect = velocity[0] * sixth_order_stencil(field, 1) + velocity[1] * wall_slope(field) + velocity[2] * sixth_order_stencil(field, 2)
        moved_field = field - step_size * advect
        predicted.append(moved_field)
        solutions.append(line_solve(moved_field, lower_coef, center_coef, upper_coefficient))
    return jnp.stack(predicted), jnp.stack(solutions)
```

```python
import jax
import jax.numpy as jnp
from jax import lax
from jax.experimental import pallas as pl
from jax.experimental.pallas import tpu as pltpu
from jax.sharding import PartitionSpec as P

step_size = 0.5
scale = step_size / 60.0
f32 = jnp.float32
VMEM_SPEC = pl.BlockSpec(memory_space=pltpu.VMEM)
HBM_SPEC = pl.BlockSpec(memory_space=pltpu.HBM)
LIMIT = 12 << 20
hops = (2, 6, 4)


def ring(count, shift):
    return [(i, (i + shift) % count) for i in range(count)]


def call(kernel, outs, in_specs, out_specs, scratch, name, args, cost, aliases=None):
    flops, moved = cost
    return pl.pallas_call(
        kernel,
        out_shape=outs,
        in_specs=in_specs,
        out_specs=out_specs,
        scratch_shapes=scratch,
        name=name,
        input_output_aliases=aliases or {},
        cost_estimate=pl.CostEstimate(flops=flops, bytes_accessed=moved, transcendentals=0),
        compiler_params=pltpu.CompilerParams(vmem_limit_bytes=LIMIT),
    )(*args)


def edge_rows(v_ref, low, high, sems):
    copies = []
    for c in range(3):
        for e in range(3):
            copies.append(pltpu.make_async_copy(v_ref.at[c, :, 13 + e], high.at[c, e], sems.at[c * 3 + e]))
            copies.append(pltpu.make_async_copy(v_ref.at[c, :, e], low.at[c, e], sems.at[9 + c * 3 + e]))
    for copy in copies:
        copy.start()
    for copy in copies:
        copy.wait()


def stage(v_ref, after, padded, z_edges, y_first, y_last, sems):
    copies = []
    for part in range(4):
        for c in range(3):
            rows = pl.ds(part * 768, 768)
            copies.append(
                pltpu.make_async_copy(
                    v_ref.at[c, rows], padded.at[c, pl.ds(16 + part * 768, 768)], sems.at[part * 3 + c]
                )
            )
    for copy in copies:
        copy.start()
    for c in range(3):
        padded[c, 0:16] = jnp.zeros((16, 128), f32)
        padded[c, 3088:3104] = jnp.zeros((16, 128), f32)
    lane = lax.broadcasted_iota(jnp.int32, (8, 128), 1)
    for part in range(4):
        for c in range(3):
            copies[part * 3 + c].wait()

        def body(step, carry):
            for u in range(2):
                t = part * 6 + step * 2 + u
                for c in range(3):
                    pieces = []
                    for i in range(16):
                        f = padded[c, pl.ds(pl.multiple_of(16 + t * 128 + i * 8, 8), 8), :]
                        here = (lane >= 8 * i) & (lane < 8 * i + 8)
                        pieces.append(jnp.where(here, pltpu.roll(f, 8 * i + 3, 1), 0.0))
                    while len(pieces) > 1:
                        pieces = [pieces[k] + pieces[k + 1] for k in range(0, len(pieces), 2)]
                    z_edges[pl.ds(pl.multiple_of(c * 192 + t * 8, 8), 8), :] = pieces[0]
            return carry

        lax.fori_loop(0, 3, body, 0)
    for c in range(3):
        y_first[c] = padded[c, 16:32]
        y_last[c] = padded[c, 3072:3088]


def shifted(value, distance, fill):
    rows, lanes = value.shape
    lane = lax.broadcasted_iota(jnp.int32, value.shape, 1)
    row = lax.broadcasted_iota(jnp.int32, value.shape, 0)
    flat = row * lanes + lane
    whole, part = divmod(abs(distance), lanes)
    if distance > 0:
        out = pltpu.roll(value, whole, 0) if whole else value
        if part:
            out = pltpu.roll(out, part, 1)
            out = jnp.where(lane < part, pltpu.roll(out, 1, 0), out)
        return jnp.where(flat < distance, fill, out)
    out = pltpu.roll(value, rows - whole, 0) if whole else value
    if part:
        out = pltpu.roll(out, lanes - part, 1)
        out = jnp.where(lane >= lanes - part, pltpu.roll(out, rows - 1, 0), out)
    return jnp.where(flat >= rows * lanes + distance, fill, out)


def homogeneous(nu_ref, after, p_ref, q_ref, table, column):
    row = lax.broadcasted_iota(jnp.int32, (16, 128), 0)
    lane = lax.broadcasted_iota(jnp.int32, (16, 128), 1)
    table[...] = jnp.ones((16, 128), f32)
    table[0:12] = nu_ref[...]
    low_face = table[...]
    high_face = shifted(low_face, -1, 1.0)
    high_face = jnp.where((row == 11) & (lane == 127), low_face, high_face)

    def products(face, towards):
        r = jnp.where(row < 12, 1.0 / face, 0.0)
        m = [1.0 + r, r, jnp.where(row < 12, 1.0, 0.0), jnp.ones((16, 128), f32)]
        k = 1
        while k < 1536:
            o = [shifted(v, towards * k, fill) for v, fill in zip(m, (1.0, 0.0, 0.0, 1.0))]
            m = [
                m[0] * o[0] + m[1] * o[2],
                m[0] * o[1] + m[1] * o[3],
                m[2] * o[0] + m[3] * o[2],
                m[2] * o[1] + m[3] * o[3],
            ]
            k *= 2
        return m, r

    before, r_low = products(low_face, 1)
    after_it, r_high = products(high_face, -1)
    p, flux = before[1], before[3]
    last = p + r_high * (flux + p)
    wronskian = jnp.broadcast_to(last[11:12, 127:128], (16, 128))
    place = lax.axis_index("wall")
    first = (place * 3) // 2
    skip = (place % 2) * 64
    sub = lax.broadcasted_iota(jnp.int32, (128, 128), 0)
    across = lax.broadcasted_iota(jnp.int32, (128, 128), 1)
    for values, out in ((p, p_ref), (after_it[1] / wronskian, q_ref)):
        table[...] = values
        for half in range(2):
            line = jnp.broadcast_to(table[pl.ds(first + half, 1), :], (128, 128))
            turned = jnp.sum(jnp.where(sub == across, line, 0.0), axis=1, keepdims=True)
            column[half * 128 : half * 128 + 128] = jnp.broadcast_to(turned, (128, 128))
        out[...] = column[pl.ds(pl.multiple_of(skip, 64), 192), :]


def interior(padded, pred):
    sub = lax.broadcasted_iota(jnp.int32, (8, 128), 0)
    source = lax.broadcasted_iota(jnp.int32, (256, 128), 0) % 128
    target = lax.broadcasted_iota(jnp.int32, (256, 128), 1)
    apart = source - target
    band = jnp.zeros((256, 128), f32)
    for m, weight in ((1, 45.0), (2, -9.0), (3, 1.0)):
        band = jnp.where(apart == m, weight, jnp.where(apart == -m, -weight, band))
    band = band.astype(jnp.bfloat16)

    def body(i, carry):
        base = 16 + i * 128

        def part(comp, offset):
            return padded[comp, pl.ds(base + offset, 8), :]

        def aligned(comp, offset, count):
            return padded[comp, pl.ds(pl.multiple_of(base + offset, 8), count), :]

        speeds = [
            (aligned(0, 8 * h, 8) * scale, aligned(1, 8 * h, 8) * (0.5 * step_size), aligned(2, 8 * h, 8) * scale)
            for h in range(16)
        ]
        for c in range(3):
            f = aligned(c, 0, 128)
            upper = f.astype(jnp.bfloat16)
            lower = (f - upper.astype(f32)).astype(jnp.bfloat16)
            slope_z = jnp.dot(jnp.concatenate([upper, lower], axis=1), band, preferred_element_type=f32)
            for h in range(16):
                slope_x = None
                for m, weight in ((1, 45.0), (2, -9.0), (3, 1.0)):
                    up = part(c, 8 * h + m)
                    down = part(c, 8 * h - m)
                    if h % 2:
                        up = jnp.where(sub < 8 - m, up, 0.0)
                    else:
                        down = jnp.where(sub < m, 0.0, down)
                    term = up - down
                    term = weight * term if weight != 1.0 else term
                    slope_x = term if m == 1 else slope_x + term
                slope_y = aligned(c, 16 + 8 * h, 8) - aligned(c, 8 * h - 16, 8)
                v0, v1, v2 = speeds[h]
                advect = v0 * slope_x + v1 * slope_y + v2 * slope_z[8 * h : 8 * h + 8]
                pred[c, pl.ds(pl.multiple_of(i * 128 + 8 * h, 8), 8), :] = f[8 * h : 8 * h + 8] - advect
        return carry

    lax.fori_loop(0, 24, body, 0)


def patch(pred_in, padded, z_edges, z_next, z_prev, below, above, p_ref, q_ref, pred, a_ref, b_ref, change):
    lane = lax.broadcasted_iota(jnp.int32, (8, 128), 1)
    outer = (lane < 3) | (lane >= 125)
    place = lax.broadcasted_iota(jnp.int32, (192, 128), 1) & 7
    for c in range(3):
        rows = slice(c * 192, c * 192 + 192)
        n = z_next[rows]
        up = pltpu.roll(n, 125, 1)
        up -= jnp.where(place >= 1, 9.0 * pltpu.roll(n, 126, 1), 0.0)
        up += jnp.where(place >= 2, 45.0 * pltpu.roll(n, 127, 1), 0.0)
        n = z_prev[rows]
        down = jnp.where(place <= 4, 9.0 * pltpu.roll(n, 2, 1), 0.0) - pltpu.roll(n, 3, 1)
        down -= jnp.where(place <= 3, 45.0 * pltpu.roll(n, 1, 1), 0.0)
        change[rows] = jnp.where(place < 3, up, down) * (z_edges[384:576] * scale)

    def body(t, carry):
        carry = list(carry)
        for c in range(3):
            packed = change[pl.ds(pl.multiple_of(c * 192 + t * 8, 8), 8), :]
            for i in range(8):
                p = p_ref[pl.ds(t * 8 + i, 1), :]
                q = q_ref[pl.ds(t * 8 + i, 1), :]
                for h in range(2):
                    k = 8 * (2 * i + h) + 3
                    back = jnp.where(outer, pltpu.roll(packed, 128 - k, 1), 0.0)
                    rows = pl.ds(pl.multiple_of(t * 128 + i * 16 + h * 8, 8), 8)
                    now = pred_in[c, rows, :] - back
                    pred[c, rows, :] = now
                    carry[c * 2 + h] = carry[c * 2 + h] + p * now
                    carry[6 + c * 2 + h] = carry[6 + c * 2 + h] + q * now
        return tuple(carry)

    sums = lax.fori_loop(0, 24, body, tuple(jnp.zeros((8, 128), f32) for _ in range(12)))
    for c in range(3):
        low = (0.5 * step_size) * padded[1, 16:32] * below[c]
        high = (0.5 * step_size) * padded[1, 3072:3088] * above[c]
        pred[c, 0:16] += low
        pred[c, 3056:3072] -= high
        for h in range(2):
            at = slice(c * 16 + h * 8, c * 16 + h * 8 + 8)
            half = slice(h * 8, h * 8 + 8)
            a_ref[at] = sums[c * 2 + h] + p_ref[0:1] * low[half] - p_ref[191:192] * high[half]
            b_ref[at] = sums[6 + c * 2 + h] + q_ref[0:1] * low[half] - q_ref[191:192] * high[half]


def faces(got_low, got_high, own_low, own_high, p_ref, q_ref, a_in, b_in, outer, both):
    both[0] = a_in[...]
    both[1] = b_in[...]
    for c in range(3):

        def body(i, carry):
            out = list(carry)
            for u in range(2):
                at = pl.ds(pl.multiple_of(i * 16 + u * 8, 8), 8)
                m3, m2, m1 = (got_low[c, j, at, :] for j in range(3))
                p1, p2, p3 = (got_high[c, j, at, :] for j in range(3))
                slopes = (
                    9.0 * m2 - 45.0 * m1 - m3,
                    9.0 * m1 - m2,
                    -m1,
                    p1,
                    p2 - 9.0 * p1,
                    45.0 * p1 - 9.0 * p2 + p3,
                )
                p = p_ref[at, :]
                q = q_ref[at, :]
                for e in range(6):
                    along = own_low[0, e, at, :] if e < 3 else own_high[0, e - 3, at, :]
                    change = along * slopes[e] * (-scale)
                    outer[c, e, at, :] = change
                    out[e] = out[e] + p * change
                    out[6 + e] = out[6 + e] + q * change
            return tuple(out)

        sums = lax.fori_loop(0, 12, body, tuple(jnp.zeros((8, 128), f32) for _ in range(12)))
        for e in range(6):
            x = e if e < 3 else e + 10
            row = pl.ds(c * 16 + x, 1)
            both[0, row, :] += jnp.sum(sums[e], axis=0, keepdims=True)
            both[1, row, :] += jnp.sum(sums[6 + e], axis=0, keepdims=True)


def local_lines(pred, outer, p_ref, q_ref, out, local, spread, full, sems):
    copies = []
    for c in range(3):

        def clear(i, carry):
            for u in range(8):
                spread[pl.ds(pl.multiple_of(i * 64 + u * 8, 8), 8), :] = jnp.zeros((8, 128), f32)
            return carry

        if c == 0:
            lax.fori_loop(0, 48, clear, 0)

        def widen(i, carry):
            for e in range(6):
                x = e if e < 3 else e + 10
                spread[pl.ds(i * 128 + x, 8, stride=16), :] = outer[c, e, pl.ds(pl.multiple_of(i * 8, 8), 8), :]
            return carry

        lax.fori_loop(0, 24, widen, 0)

        def body(i, carry):
            s, t = carry
            for u in range(8):
                y = i * 8 + u
                p = p_ref[pl.ds(y, 1), :]
                q = q_ref[pl.ds(y, 1), :]
                at = pl.ds(pl.multiple_of(y * 16, 16), 16)
                r = pred[c, at, :] + spread[at, :]
                full[c, at, :] = r
                s = s + p * r
                t = t + q * r
                local[c, at, :] = q * s - p * t
            return s, t

        lax.fori_loop(0, 24, body, tuple(jnp.zeros((16, 128), f32) for _ in range(2)))
        copy = pltpu.make_async_copy(full.at[c], out.at[c], sems.at[c])
        copy.start()
        copies.append(copy)
    for copy in copies:
        copy.wait()


def pairs(both, other, *sent):
    place = lax.axis_index("wall")
    for k, out in zip(hops, sent):
        side = jnp.where(place + k < 8, 0, 1)
        out[...] = both[side] + other[side]


def finish(local, p_ref, q_ref, both, other, got_0, got_1, got_2, out, staged, sems):
    place = lax.axis_index("wall")
    second = place % 2 == 1
    low_all = jnp.where(second, other[0], 0.0)
    high_all = both[1] + jnp.where(second, 0.0, other[1])
    for k, got in zip(hops, (got_0, got_1, got_2)):
        value = got[...]
        low_all += jnp.where(place >= k, value, 0.0)
        high_all += jnp.where(place >= k, 0.0, value)
    low = [low_all[c * 16 : c * 16 + 16] for c in range(3)]
    high = [high_all[c * 16 : c * 16 + 16] for c in range(3)]
    copies = []
    for part in range(6):

        def body(i, carry):
            for u in range(4):
                y = part * 32 + i * 4 + u
                p = p_ref[pl.ds(y, 1), :]
                q = q_ref[pl.ds(y, 1), :]
                at = pl.ds(pl.multiple_of(y * 16, 16), 16)
                for c in range(3):
                    staged[c, at, :] = local[c, at, :] + (q * low[c] + p * high[c])
            return carry

        lax.fori_loop(0, 8, body, 0)
        for c in range(3):
            rows = pl.ds(part * 512, 512)
            copy = pltpu.make_async_copy(staged.at[c, rows], out.at[c, rows], sems.at[part * 3 + c])
            copy.start()
            copies.append(copy)
    for copy in copies:
        copy.wait()


def on_device(velocity, viscosity):
    groups = lax.axis_size("wall")
    spans = lax.axis_size("span")
    streams = lax.axis_size("stream")
    DMA = pltpu.SemaphoreType.DMA
    shape = jax.ShapeDtypeStruct
    block = (3, 3072, 128)

    by_row = pltpu.with_memory_space_constraint(velocity.reshape(3, 192, 16, 1, 128), pltpu.HBM)
    edge = shape((3, 3, 192, 1, 128), f32)
    own_low, own_high = call(
        edge_rows, (edge, edge), [HBM_SPEC], (VMEM_SPEC,) * 2, [DMA((18,))], "edge_rows", (by_row,), (0, 3600000)
    )
    own_low = own_low.reshape(3, 3, 192, 128)
    own_high = own_high.reshape(3, 3, 192, 128)
    got_low = lax.ppermute(own_high, "stream", ring(streams, 1))
    got_high = lax.ppermute(own_low, "stream", ring(streams, -1))

    flat = pltpu.with_memory_space_constraint(velocity.reshape(block), pltpu.HBM)
    packed = shape((576, 128), f32)
    layer = shape((3, 16, 128), f32)
    padded, z_edges, y_first, y_last = call(
        stage,
        (shape((3, 3104, 128), f32), packed, layer, layer),
        [HBM_SPEC, pl.BlockSpec(memory_space=pl.ANY)],
        (VMEM_SPEC,) * 4,
        [DMA((12,))],
        "stage",
        (flat, own_low),
        (9000000, 10000000),
    )
    z_next = lax.ppermute(z_edges, "span", ring(spans, -1))
    z_prev = lax.ppermute(z_edges, "span", ring(spans, 1))
    below = lax.ppermute(y_last, "wall", [(i, i + 1) for i in range(groups - 1)])
    above = lax.ppermute(y_first, "wall", [(i + 1, i) for i in range(groups - 1)])

    own_rows = shape((192, 128), f32)
    p, q = call(
        homogeneous,
        (own_rows, own_rows),
        [VMEM_SPEC, pl.BlockSpec(memory_space=pl.ANY)],
        (VMEM_SPEC,) * 2,
        [pltpu.VMEM((16, 128), f32), pltpu.VMEM((256, 128), f32)],
        "homogeneous",
        (viscosity.reshape(12, 128), z_edges),
        (3000000, 32768),
    )

    sums = shape((48, 128), f32)
    pred = call(
        interior, shape(block, f32), [VMEM_SPEC], VMEM_SPEC, [], "interior", (padded,), (60000000, 10000000)
    )
    pred, a, b = call(
        patch,
        (shape(block, f32), sums, sums),
        [VMEM_SPEC] * 9,
        (VMEM_SPEC,) * 3,
        [pltpu.VMEM((576, 128), f32)],
        "patch",
        (pred, padded, z_edges, z_next, z_prev, below, above, p, q),
        (20000000, 10000000),
        {0: 0},
    )
    outer, both = call(
        faces,
        (shape((3, 6, 192, 128), f32), shape((2, 48, 128), f32)),
        [VMEM_SPEC] * 8,
        (VMEM_SPEC,) * 2,
        [],
        "faces",
        (got_low, got_high, own_low, own_high, p, q, a, b),
        (5000000, 5000000),
    )

    other = lax.ppermute(both, "wall", [(i, i ^ 1) for i in range(groups)])
    sent = call(
        pairs, (sums,) * 3, [VMEM_SPEC] * 2, (VMEM_SPEC,) * 3, [], "pairs", (both, other), (40000, 150000)
    )
    got = [lax.ppermute(value, "wall", ring(groups, k)) for k, value in zip(hops, sent)]

    predictor, local = call(
        local_lines,
        (pltpu.HBM(block, f32), shape(block, f32)),
        [VMEM_SPEC] * 4,
        (HBM_SPEC, VMEM_SPEC),
        [pltpu.VMEM((3072, 128), f32), pltpu.VMEM(block, f32), DMA((3,))],
        "local_lines",
        (pred, outer, p, q),
        (9000000, 14000000),
    )
    velocity_new = call(
        finish,
        pltpu.HBM(block, f32),
        [VMEM_SPEC] * 8,
        HBM_SPEC,
        [pltpu.VMEM(block, f32), DMA((18,))],
        "finish",
        (local, p, q, both, other, *got),
        (5000000, 10000000),
    )
    return predictor.reshape(velocity.shape), velocity_new.reshape(velocity.shape)


def solution(mesh):
    return jax.shard_map(
        on_device,
        mesh=mesh,
        in_specs=(P(None, "wall", "stream", "span"), P()),
        out_specs=(P(None, "wall", "stream", "span"), P(None, "wall", "stream", "span")),
        check_vma=False,
    )
```

```python
import functools

import jax
import jax.numpy as jnp
from jax import lax
from jax.experimental import pallas as pl
from jax.experimental.pallas import tpu as pltpu
from jax.sharding import PartitionSpec as P

step_size = 0.5
scale = step_size / 60.0
f32 = jnp.float32
VMEM_SPEC = pl.BlockSpec(memory_space=pltpu.VMEM)
HBM_SPEC = pl.BlockSpec(memory_space=pltpu.HBM)
LIMIT = 12 << 20
hops = (4, 2, 6)


def ring(count, shift):
    return [(i, (i + shift) % count) for i in range(count)]


def call(kernel, outs, in_specs, out_specs, scratch, name, args, cost, aliases=None):
    flops, moved = cost
    return pl.pallas_call(
        kernel,
        out_shape=outs,
        in_specs=in_specs,
        out_specs=out_specs,
        scratch_shapes=scratch,
        name=name,
        input_output_aliases=aliases or {},
        cost_estimate=pl.CostEstimate(flops=flops, bytes_accessed=moved, transcendentals=0),
        compiler_params=pltpu.CompilerParams(vmem_limit_bytes=LIMIT),
    )(*args)


def edge_rows(v_ref, low, high, sems):
    copies = []
    for c in range(3):
        to = pl.ds(4 + 192 * c, 192)
        copies.append(pltpu.make_async_copy(v_ref.at[c, :, 13:16], high.at[to], sems.at[c]))
        copies.append(pltpu.make_async_copy(v_ref.at[c, :, 0:3], low.at[to], sems.at[3 + c]))
    for copy in copies:
        copy.start()
    for ref in (low, high):
        ref[0:4] = jnp.zeros((4, 3, 1, 128), f32)
        ref[580:584] = jnp.zeros((4, 3, 1, 128), f32)
    for copy in copies:
        copy.wait()


def stage(v_ref, after, z_edges):
    lane = lax.broadcasted_iota(jnp.int32, (8, 128), 1)

    def body(step, carry):
        for u in range(2):
            t = step * 2 + u
            for c in range(3):
                pieces = []
                for i in range(16):
                    f = v_ref[c, pl.ds(pl.multiple_of(t * 128 + i * 8, 8), 8), :]
                    here = (lane >= 8 * i) & (lane < 8 * i + 8)
                    pieces.append(jnp.where(here, pltpu.roll(f, 8 * i + 3, 1), 0.0))
                while len(pieces) > 1:
                    pieces = [pieces[k] + pieces[k + 1] for k in range(0, len(pieces), 2)]
                z_edges[pl.ds(pl.multiple_of(c * 192 + t * 8, 8), 8), :] = pieces[0]
        return carry

    lax.fori_loop(0, 12, body, 0)


def shifted(value, distance, fill):
    rows, lanes = value.shape
    lane = lax.broadcasted_iota(jnp.int32, value.shape, 1)
    row = lax.broadcasted_iota(jnp.int32, value.shape, 0)
    flat = row * lanes + lane
    whole, part = divmod(abs(distance), lanes)
    if distance > 0:
        out = pltpu.roll(value, whole, 0) if whole else value
        if part:
            out = pltpu.roll(out, part, 1)
            out = jnp.where(lane < part, pltpu.roll(out, 1, 0), out)
        return jnp.where(flat < distance, fill, out)
    out = pltpu.roll(value, rows - whole, 0) if whole else value
    if part:
        out = pltpu.roll(out, lanes - part, 1)
        out = jnp.where(lane >= lanes - part, pltpu.roll(out, rows - 1, 0), out)
    return jnp.where(flat >= rows * lanes + distance, fill, out)


def homogeneous(nu_ref, after, p_ref, q_ref, table, column):
    row = lax.broadcasted_iota(jnp.int32, (16, 128), 0)
    lane = lax.broadcasted_iota(jnp.int32, (16, 128), 1)
    table[...] = jnp.ones((16, 128), f32)
    table[0:12] = nu_ref[...]
    low_face = table[...]
    high_face = shifted(low_face, -1, 1.0)
    high_face = jnp.where((row == 11) & (lane == 127), low_face, high_face)

    def products(face, towards):
        r = jnp.where(row < 12, 1.0 / face, 0.0)
        m = [1.0 + r, r, jnp.where(row < 12, 1.0, 0.0), jnp.ones((16, 128), f32)]
        k = 1
        while k < 1536:
            o = [shifted(v, towards * k, fill) for v, fill in zip(m, (1.0, 0.0, 0.0, 1.0))]
            m = [
                m[0] * o[0] + m[1] * o[2],
                m[0] * o[1] + m[1] * o[3],
                m[2] * o[0] + m[3] * o[2],
                m[2] * o[1] + m[3] * o[3],
            ]
            k *= 2
        return m, r

    before, r_low = products(low_face, 1)
    after_it, r_high = products(high_face, -1)
    p, flux = before[1], before[3]
    last = p + r_high * (flux + p)
    wronskian = jnp.broadcast_to(last[11:12, 127:128], (16, 128))
    place = lax.axis_index("wall")
    first = (place * 3) // 2
    skip = (place % 2) * 64
    sub = lax.broadcasted_iota(jnp.int32, (128, 128), 0)
    across = lax.broadcasted_iota(jnp.int32, (128, 128), 1)
    for values, out in ((p, p_ref), (after_it[1] / wronskian, q_ref)):
        table[...] = values
        for half in range(2):
            line = jnp.broadcast_to(table[pl.ds(first + half, 1), :], (128, 128))
            turned = jnp.sum(jnp.where(sub == across, line, 0.0), axis=1, keepdims=True)
            column[half * 128 : half * 128 + 128] = jnp.broadcast_to(turned, (128, 128))
        out[...] = column[pl.ds(pl.multiple_of(skip, 64), 192), :]


def interior(v_ref, after, pred, y_first, y_last):
    sub = lax.broadcasted_iota(jnp.int32, (8, 128), 0)
    source = lax.broadcasted_iota(jnp.int32, (256, 128), 0) % 128
    target = lax.broadcasted_iota(jnp.int32, (256, 128), 1)
    apart = source - target
    band = jnp.zeros((256, 128), f32)
    for m, weight in ((1, 45.0), (2, -9.0), (3, 1.0)):
        band = jnp.where(apart == m, weight, jnp.where(apart == -m, -weight, band))
    band = band.astype(jnp.bfloat16)

    def eight_rows(i, first, last):
        base = i * 128

        def part(comp, offset):
            return v_ref[comp, pl.ds(base + offset, 8), :]

        def aligned(comp, offset, count):
            at = base + offset
            return v_ref[comp, pl.ds(at if isinstance(at, int) else pl.multiple_of(at, 8), count), :]

        speeds = [
            (aligned(0, 8 * h, 8) * scale, aligned(1, 8 * h, 8) * (0.5 * step_size), aligned(2, 8 * h, 8) * scale)
            for h in range(16)
        ]
        for c in range(3):
            f = aligned(c, 0, 128)
            upper = f.astype(jnp.bfloat16)
            lower = (f - upper.astype(f32)).astype(jnp.bfloat16)
            slope_z = jnp.dot(jnp.concatenate([upper, lower], axis=1), band, preferred_element_type=f32)
            for h in range(16):
                here = f[8 * h : 8 * h + 8]
                slope_x = None
                for m, weight in ((1, 45.0), (2, -9.0), (3, 1.0)):
                    up = pltpu.roll(here, 8 - m, 0) if last and h == 15 else part(c, 8 * h + m)
                    down = pltpu.roll(here, m, 0) if first and h == 0 else part(c, 8 * h - m)
                    if h % 2:
                        up = jnp.where(sub < 8 - m, up, 0.0)
                    else:
                        down = jnp.where(sub < m, 0.0, down)
                    term = up - down
                    term = weight * term if weight != 1.0 else term
                    slope_x = term if m == 1 else slope_x + term
                if first and h < 2:
                    slope_y = aligned(c, 16 + 8 * h, 8)
                elif last and h >= 14:
                    slope_y = -aligned(c, 8 * h - 16, 8)
                else:
                    slope_y = aligned(c, 16 + 8 * h, 8) - aligned(c, 8 * h - 16, 8)
                v0, v1, v2 = speeds[h]
                advect = v0 * slope_x + v1 * slope_y + v2 * slope_z[8 * h : 8 * h + 8]
                at = base + 8 * h
                pred[c, pl.ds(at if isinstance(at, int) else pl.multiple_of(at, 8), 8), :] = here - advect

    def body(i, carry):
        eight_rows(i, False, False)
        return carry

    eight_rows(0, True, False)
    lax.fori_loop(1, 23, body, 0)
    eight_rows(23, False, True)
    for c in range(3):
        y_first[c] = v_ref[c, 0:16]
        y_last[c] = v_ref[c, 3056:3072]


def patch(pred_in, z_edges, z_next, z_prev, after, pred, change):
    lane = lax.broadcasted_iota(jnp.int32, (8, 128), 1)
    outer = (lane < 3) | (lane >= 125)
    place = lax.broadcasted_iota(jnp.int32, (192, 128), 1) & 7
    for c in range(3):
        rows = slice(c * 192, c * 192 + 192)
        n = z_next[rows]
        up = pltpu.roll(n, 125, 1)
        up -= jnp.where(place >= 1, 9.0 * pltpu.roll(n, 126, 1), 0.0)
        up += jnp.where(place >= 2, 45.0 * pltpu.roll(n, 127, 1), 0.0)
        n = z_prev[rows]
        down = jnp.where(place <= 4, 9.0 * pltpu.roll(n, 2, 1), 0.0) - pltpu.roll(n, 3, 1)
        down -= jnp.where(place <= 3, 45.0 * pltpu.roll(n, 1, 1), 0.0)
        change[rows] = jnp.where(place < 3, up, down) * (z_edges[384:576] * scale)

    def body(t, carry):
        for c in range(3):
            packed = change[pl.ds(pl.multiple_of(c * 192 + t * 8, 8), 8), :]
            rows = pl.ds(pl.multiple_of(t * 128, 128), 128)
            before = pred_in[c, rows, :]
            now = []
            for i in range(16):
                back = jnp.where(outer, pltpu.roll(packed, 125 - 8 * i, 1), 0.0)
                now.append(before[i * 8 : i * 8 + 8] - back)
            pred[c, rows, :] = jnp.concatenate(now, axis=0)
        return carry

    lax.fori_loop(0, 24, body, 0)


def arrived(got, out):
    pass


def faces(pred_in, v_ref, got_low, got_high, below, above, p_ref, q_ref, pred, both, out, sems):
    sub = lax.broadcasted_iota(jnp.int32, (8, 128), 0)
    low_weights = [jnp.where(sub <= 2 - k, w * scale, 0.0) for k, w in enumerate((-1.0, 9.0, -45.0))]
    high_weights = [jnp.where(sub >= 5 + k, w * scale, 0.0) for k, w in enumerate((1.0, -9.0, 45.0))]

    def eight_rows(i, carry):
        carry = list(carry)
        for c in range(3):
            rows = pl.ds(pl.multiple_of(i * 128, 128), 128)
            before = pred_in[c, rows, :]
            along = v_ref[0, rows, :]
            now = []
            for y in range(8):
                at = 12 + c * 576 + i * 24 + 3 * y
                low = [w * got_low[pl.ds(at + k, 8), :] for k, w in enumerate(low_weights)]
                high = [w * got_high[pl.ds(at - 5 - k, 8), :] for k, w in enumerate(high_weights)]
                p = p_ref[pl.ds(i * 8 + y, 1), :]
                q = q_ref[pl.ds(i * 8 + y, 1), :]
                for h, slope in enumerate((low, high)):
                    here = slice(y * 16 + h * 8, y * 16 + h * 8 + 8)
                    r = before[here] - along[here] * (slope[0] + slope[1] + slope[2])
                    now.append(r)
                    carry[c * 2 + h] = carry[c * 2 + h] + p * r
                    carry[6 + c * 2 + h] = carry[6 + c * 2 + h] + q * r
            pred[c, rows, :] = jnp.concatenate(now, axis=0)
        return tuple(carry)

    sums = lax.fori_loop(0, 12, eight_rows, tuple(jnp.zeros((8, 128), f32) for _ in range(12)))
    lows = [(0.5 * step_size) * v_ref[1, 0:16, :] * below[c] for c in range(3)]
    highs = [(0.5 * step_size) * v_ref[1, 3056:3072, :] * above[c] for c in range(3)]
    copies = []
    for c in range(3):
        pred[c, 0:16] += lows[c]
        copies.append(pltpu.make_async_copy(pred.at[c, 0:1536], out.at[c, 0:1536], sems.at[c]))
        copies[c].start()
    sums = lax.fori_loop(12, 24, eight_rows, sums)
    for c in range(3):
        pred[c, 3056:3072] -= highs[c]
        for h in range(2):
            at = slice(c * 16 + h * 8, c * 16 + h * 8 + 8)
            half = slice(h * 8, h * 8 + 8)
            k = c * 2 + h
            both[0, at] = sums[k] + p_ref[0:1] * lows[c][half] - p_ref[191:192] * highs[c][half]
            both[1, at] = sums[6 + k] + q_ref[0:1] * lows[c][half] - q_ref[191:192] * highs[c][half]
    for copy in copies:
        copy.wait()


def written(start, count, pred, onto, out, token, sems):
    token[...] = jnp.zeros_like(token)
    rows = pl.ds(start, count)
    copies = [pltpu.make_async_copy(pred.at[c, rows], out.at[c, rows], sems.at[c]) for c in range(3)]
    for copy in copies:
        copy.start()
    for copy in copies:
        copy.wait()


def pairs(both, other, after, *sent):
    place = lax.axis_index("wall")
    for k, out in zip(hops, sent):
        side = jnp.where(place + k < 8, 0, 1)
        out[...] = both[side] + other[side]


def finish(pred, p_ref, q_ref, both, other, got_0, got_1, got_2, out, staged, sems):
    place = lax.axis_index("wall")
    second = place % 2 == 1
    low = jnp.where(second, other[0], 0.0)
    high = both[1] + jnp.where(second, 0.0, other[1])
    for k, got in zip(hops, (got_0, got_1, got_2)):
        value = got[...]
        low += jnp.where(place >= k, value, 0.0)
        high += jnp.where(place >= k, 0.0, value)
    carry = tuple(part[c * 16 : c * 16 + 16] for part in (low, high) for c in range(3))
    copies = []
    for part in range(6):

        def body(i, carry):
            carry = list(carry)
            for c in range(3):
                rows = pl.ds(pl.multiple_of(part * 512 + i * 128, 128), 128)
                r = pred[c, rows, :]
                now = []
                for u in range(8):
                    y = part * 32 + i * 8 + u
                    p = p_ref[pl.ds(y, 1), :]
                    q = q_ref[pl.ds(y, 1), :]
                    here = r[u * 16 : u * 16 + 16]
                    carry[c] = carry[c] + p * here
                    carry[3 + c] = carry[3 + c] - q * here
                    now.append(q * carry[c] + p * carry[3 + c])
                staged[c, rows, :] = jnp.concatenate(now, axis=0)
            return tuple(carry)

        carry = lax.fori_loop(0, 4, body, carry)
        for c in range(3):
            rows = pl.ds(part * 512, 512)
            copy = pltpu.make_async_copy(staged.at[c, rows], out.at[c, rows], sems.at[part * 3 + c])
            copy.start()
            copies.append(copy)
    for copy in copies:
        copy.wait()


def on_device(velocity, viscosity):
    groups = lax.axis_size("wall")
    spans = lax.axis_size("span")
    streams = lax.axis_size("stream")
    DMA = pltpu.SemaphoreType.DMA
    shape = jax.ShapeDtypeStruct
    block = (3, 3072, 128)

    ANY = pl.BlockSpec(memory_space=pl.ANY)
    by_row = pltpu.with_memory_space_constraint(velocity.reshape(3, 192, 16, 1, 128), pltpu.HBM)
    edge = shape((584, 3, 1, 128), f32)
    own_low, own_high = call(
        edge_rows, (edge, edge), [HBM_SPEC], (VMEM_SPEC,) * 2, [DMA((6,))], "edge_rows", (by_row,), (0, 3600000)
    )
    got_low = lax.ppermute(own_high.reshape(1752, 128), "stream", ring(streams, 1))
    got_high = lax.ppermute(own_low.reshape(1752, 128), "stream", ring(streams, -1))

    flat = velocity.reshape(block)
    layer = shape((3, 16, 128), f32)
    z_edges = call(
        stage,
        shape((576, 128), f32),
        [VMEM_SPEC, ANY],
        VMEM_SPEC,
        [],
        "stage",
        (flat, own_low),
        (9000000, 10000000),
    )
    z_next = lax.ppermute(z_edges, "span", ring(spans, -1))
    z_prev = lax.ppermute(z_edges, "span", ring(spans, 1))
    sums = shape((48, 128), f32)
    pred, y_first, y_last = call(
        interior,
        (shape(block, f32), layer, layer),
        [VMEM_SPEC, ANY],
        (VMEM_SPEC,) * 3,
        [],
        "interior",
        (flat, z_edges),
        (60000000, 10000000),
    )
    below = lax.ppermute(y_last, "wall", [(i, i + 1) for i in range(groups - 1)])
    above = lax.ppermute(y_first, "wall", [(i + 1, i) for i in range(groups - 1)])

    own_rows = shape((192, 128), f32)
    p, q = call(
        homogeneous,
        (own_rows, own_rows),
        [VMEM_SPEC, ANY],
        (VMEM_SPEC,) * 2,
        [pltpu.VMEM((16, 128), f32), pltpu.VMEM((256, 128), f32)],
        "homogeneous",
        (viscosity.reshape(12, 128), y_first),
        (3000000, 32768),
    )

    pred = call(
        patch,
        shape(block, f32),
        [VMEM_SPEC] * 4 + [ANY],
        VMEM_SPEC,
        [pltpu.VMEM((576, 128), f32)],
        "patch",
        (pred, z_edges, z_next, z_prev, p),
        (20000000, 10000000),
        {0: 0},
    )
    got_low = call(
        arrived, shape(got_low.shape, f32), [VMEM_SPEC], VMEM_SPEC, [], "arrived", (got_low,), (0, 1024), {0: 0}
    )
    pred, both, predictor = call(
        faces,
        (shape(block, f32), shape((2, 48, 128), f32), pltpu.HBM(block, f32)),
        [VMEM_SPEC] * 8,
        (VMEM_SPEC, VMEM_SPEC, HBM_SPEC),
        [DMA((3,))],
        "faces",
        (pred, flat, got_low, got_high, below, above, p, q),
        (20000000, 10000000),
        {0: 0},
    )

    other = lax.ppermute(both, "wall", [(i, i ^ 1) for i in range(groups)])

    def write(onto, start, count):
        return call(
            functools.partial(written, start, count),
            (pltpu.HBM(block, f32), shape((8, 128), f32)),
            [VMEM_SPEC, HBM_SPEC],
            (HBM_SPEC, VMEM_SPEC),
            [DMA((3,))],
            "written",
            (pred, onto),
            (0, count * 3072),
            {1: 0},
        )

    predictor, after = write(predictor, 1536, 768)
    sent = call(
        pairs, (sums,) * 3, [VMEM_SPEC] * 2 + [ANY], (VMEM_SPEC,) * 3, [], "pairs", (both, other, after), (40000, 150000)
    )
    got = [lax.ppermute(value, "wall", ring(groups, k)) for k, value in zip(hops, sent)]
    predictor, after = write(predictor, 2304, 768)
    velocity_new = call(
        finish,
        pltpu.HBM(block, f32),
        [VMEM_SPEC] * 8,
        HBM_SPEC,
        [pltpu.VMEM(block, f32), DMA((18,))],
        "finish",
        (pred, p, q, both, other, *got),
        (9000000, 10000000),
    )
    return predictor.reshape(velocity.shape), velocity_new.reshape(velocity.shape)


def solution(mesh):
    return jax.shard_map(
        on_device,
        mesh=mesh,
        in_specs=(P(None, "wall", "stream", "span"), P()),
        out_specs=(P(None, "wall", "stream", "span"), P(None, "wall", "stream", "span")),
        check_vma=False,
    )
```

```python
import functools

import jax
import jax.numpy as jnp
from jax import lax
from jax.experimental import pallas as pl
from jax.experimental.pallas import tpu as pltpu
from jax.sharding import PartitionSpec as P

step_size = 0.5
scale = step_size / 60.0
f32 = jnp.float32
VMEM_SPEC = pl.BlockSpec(memory_space=pltpu.VMEM)
HBM_SPEC = pl.BlockSpec(memory_space=pltpu.HBM)
LIMIT = 12 << 20
hops = (2, 4, 6)


def ring(count, shift):
    return [(i, (i + shift) % count) for i in range(count)]


def call(kernel, outs, in_specs, out_specs, scratch, name, args, cost, aliases=None):
    flops, moved = cost
    return pl.pallas_call(
        kernel,
        out_shape=outs,
        in_specs=in_specs,
        out_specs=out_specs,
        scratch_shapes=scratch,
        name=name,
        input_output_aliases=aliases or {},
        cost_estimate=pl.CostEstimate(flops=flops, bytes_accessed=moved, transcendentals=0),
        compiler_params=pltpu.CompilerParams(vmem_limit_bytes=LIMIT),
    )(*args)


def edge_rows(v_ref, low, high, sems):
    copies = []
    for c in range(3):
        to = pl.ds(4 + 192 * c, 192)
        copies.append(pltpu.make_async_copy(v_ref.at[c, :, 13:16], high.at[to], sems.at[c]))
        copies.append(pltpu.make_async_copy(v_ref.at[c, :, 0:3], low.at[to], sems.at[3 + c]))
    for copy in copies:
        copy.start()
    for ref in (low, high):
        ref[0:4] = jnp.zeros((4, 3, 1, 128), f32)
        ref[580:584] = jnp.zeros((4, 3, 1, 128), f32)
    for copy in copies:
        copy.wait()


def stage(v_ref, after, z_edges):
    lane = lax.broadcasted_iota(jnp.int32, (8, 128), 1)

    def body(step, carry):
        for u in range(2):
            t = step * 2 + u
            for c in range(3):
                pieces = []
                for i in range(16):
                    f = v_ref[c, pl.ds(pl.multiple_of(t * 128 + i * 8, 8), 8), :]
                    here = (lane >= 8 * i) & (lane < 8 * i + 8)
                    pieces.append(jnp.where(here, pltpu.roll(f, 8 * i + 3, 1), 0.0))
                while len(pieces) > 1:
                    pieces = [pieces[k] + pieces[k + 1] for k in range(0, len(pieces), 2)]
                z_edges[pl.ds(pl.multiple_of(c * 192 + t * 8, 8), 8), :] = pieces[0]
        return carry

    lax.fori_loop(0, 12, body, 0)


def shifted(value, distance, fill):
    rows, lanes = value.shape
    lane = lax.broadcasted_iota(jnp.int32, value.shape, 1)
    row = lax.broadcasted_iota(jnp.int32, value.shape, 0)
    flat = row * lanes + lane
    whole, part = divmod(abs(distance), lanes)
    if distance > 0:
        out = pltpu.roll(value, whole, 0) if whole else value
        if part:
            out = pltpu.roll(out, part, 1)
            out = jnp.where(lane < part, pltpu.roll(out, 1, 0), out)
        return jnp.where(flat < distance, fill, out)
    out = pltpu.roll(value, rows - whole, 0) if whole else value
    if part:
        out = pltpu.roll(out, lanes - part, 1)
        out = jnp.where(lane >= lanes - part, pltpu.roll(out, rows - 1, 0), out)
    return jnp.where(flat >= rows * lanes + distance, fill, out)


def homogeneous(nu_ref, after, p_ref, q_ref, table, column):
    row = lax.broadcasted_iota(jnp.int32, (16, 128), 0)
    lane = lax.broadcasted_iota(jnp.int32, (16, 128), 1)
    table[...] = jnp.ones((16, 128), f32)
    table[0:12] = nu_ref[...]
    low_face = table[...]
    high_face = shifted(low_face, -1, 1.0)
    high_face = jnp.where((row == 11) & (lane == 127), low_face, high_face)

    def products(face, towards):
        r = jnp.where(row < 12, 1.0 / face, 0.0)
        m = [1.0 + r, r, jnp.where(row < 12, 1.0, 0.0), jnp.ones((16, 128), f32)]
        k = 1
        while k < 1536:
            o = [shifted(v, towards * k, fill) for v, fill in zip(m, (1.0, 0.0, 0.0, 1.0))]
            m = [
                m[0] * o[0] + m[1] * o[2],
                m[0] * o[1] + m[1] * o[3],
                m[2] * o[0] + m[3] * o[2],
                m[2] * o[1] + m[3] * o[3],
            ]
            k *= 2
        return m, r

    before, r_low = products(low_face, 1)
    after_it, r_high = products(high_face, -1)
    p, flux = before[1], before[3]
    last = p + r_high * (flux + p)
    wronskian = jnp.broadcast_to(last[11:12, 127:128], (16, 128))
    place = lax.axis_index("wall")
    first = (place * 3) // 2
    skip = (place % 2) * 64
    sub = lax.broadcasted_iota(jnp.int32, (128, 128), 0)
    across = lax.broadcasted_iota(jnp.int32, (128, 128), 1)
    for values, out in ((p, p_ref), (after_it[1] / wronskian, q_ref)):
        table[...] = values
        for half in range(2):
            line = jnp.broadcast_to(table[pl.ds(first + half, 1), :], (128, 128))
            turned = jnp.sum(jnp.where(sub == across, line, 0.0), axis=1, keepdims=True)
            column[half * 128 : half * 128 + 128] = jnp.broadcast_to(turned, (128, 128))
        out[...] = column[pl.ds(pl.multiple_of(skip, 64), 192), :]


def interior(v_ref, after, pred, y_first, y_last):
    sub = lax.broadcasted_iota(jnp.int32, (8, 128), 0)
    source = lax.broadcasted_iota(jnp.int32, (256, 128), 0) % 128
    target = lax.broadcasted_iota(jnp.int32, (256, 128), 1)
    apart = source - target
    band = jnp.zeros((256, 128), f32)
    for m, weight in ((1, 45.0), (2, -9.0), (3, 1.0)):
        band = jnp.where(apart == m, weight, jnp.where(apart == -m, -weight, band))
    band = band.astype(jnp.bfloat16)

    def eight_rows(i, first, last):
        base = i * 128

        def part(comp, offset):
            return v_ref[comp, pl.ds(base + offset, 8), :]

        def aligned(comp, offset, count):
            at = base + offset
            return v_ref[comp, pl.ds(at if isinstance(at, int) else pl.multiple_of(at, 8), count), :]

        speeds = [
            (aligned(0, 8 * h, 8) * scale, aligned(1, 8 * h, 8) * (0.5 * step_size), aligned(2, 8 * h, 8) * scale)
            for h in range(16)
        ]
        for c in range(3):
            f = aligned(c, 0, 128)
            upper = f.astype(jnp.bfloat16)
            lower = (f - upper.astype(f32)).astype(jnp.bfloat16)
            slope_z = jnp.dot(jnp.concatenate([upper, lower], axis=1), band, preferred_element_type=f32)
            for h in range(16):
                here = f[8 * h : 8 * h + 8]
                slope_x = None
                for m, weight in ((1, 45.0), (2, -9.0), (3, 1.0)):
                    up = pltpu.roll(here, 8 - m, 0) if last and h == 15 else part(c, 8 * h + m)
                    down = pltpu.roll(here, m, 0) if first and h == 0 else part(c, 8 * h - m)
                    if h % 2:
                        up = jnp.where(sub < 8 - m, up, 0.0)
                    else:
                        down = jnp.where(sub < m, 0.0, down)
                    term = up - down
                    term = weight * term if weight != 1.0 else term
                    slope_x = term if m == 1 else slope_x + term
                if first and h < 2:
                    slope_y = aligned(c, 16 + 8 * h, 8)
                elif last and h >= 14:
                    slope_y = -aligned(c, 8 * h - 16, 8)
                else:
                    slope_y = aligned(c, 16 + 8 * h, 8) - aligned(c, 8 * h - 16, 8)
                v0, v1, v2 = speeds[h]
                advect = v0 * slope_x + v1 * slope_y + v2 * slope_z[8 * h : 8 * h + 8]
                at = base + 8 * h
                pred[c, pl.ds(at if isinstance(at, int) else pl.multiple_of(at, 8), 8), :] = here - advect

    def body(i, carry):
        eight_rows(i, False, False)
        return carry

    eight_rows(0, True, False)
    lax.fori_loop(1, 23, body, 0)
    eight_rows(23, False, True)
    for c in range(3):
        y_first[c] = v_ref[c, 0:16]
        y_last[c] = v_ref[c, 3056:3072]


def patch(pred_in, z_edges, z_next, z_prev, after, pred, change):
    lane = lax.broadcasted_iota(jnp.int32, (8, 128), 1)
    outer = (lane < 3) | (lane >= 125)
    place = lax.broadcasted_iota(jnp.int32, (192, 128), 1) & 7
    for c in range(3):
        rows = slice(c * 192, c * 192 + 192)
        n = z_next[rows]
        up = pltpu.roll(n, 125, 1)
        up -= jnp.where(place >= 1, 9.0 * pltpu.roll(n, 126, 1), 0.0)
        up += jnp.where(place >= 2, 45.0 * pltpu.roll(n, 127, 1), 0.0)
        n = z_prev[rows]
        down = jnp.where(place <= 4, 9.0 * pltpu.roll(n, 2, 1), 0.0) - pltpu.roll(n, 3, 1)
        down -= jnp.where(place <= 3, 45.0 * pltpu.roll(n, 1, 1), 0.0)
        change[rows] = jnp.where(place < 3, up, down) * (z_edges[384:576] * scale)

    def body(t, carry):
        for c in range(3):
            packed = change[pl.ds(pl.multiple_of(c * 192 + t * 8, 8), 8), :]
            rows = pl.ds(pl.multiple_of(t * 128, 128), 128)
            before = pred_in[c, rows, :]
            now = []
            for i in range(16):
                back = jnp.where(outer, pltpu.roll(packed, 125 - 8 * i, 1), 0.0)
                now.append(before[i * 8 : i * 8 + 8] - back)
            pred[c, rows, :] = jnp.concatenate(now, axis=0)
        return carry

    lax.fori_loop(0, 24, body, 0)


def arrived(got, out):
    pass


def faces(pred_in, v_ref, got_low, got_high, below, above, p_ref, q_ref, pred, both, out, sems):
    sub = lax.broadcasted_iota(jnp.int32, (8, 128), 0)
    low_weights = [jnp.where(sub <= 2 - k, w * scale, 0.0) for k, w in enumerate((-1.0, 9.0, -45.0))]
    high_weights = [jnp.where(sub >= 5 + k, w * scale, 0.0) for k, w in enumerate((1.0, -9.0, 45.0))]

    def eight_rows(i, carry):
        carry = list(carry)
        for c in range(3):
            rows = pl.ds(pl.multiple_of(i * 128, 128), 128)
            before = pred_in[c, rows, :]
            along = v_ref[0, rows, :]
            now = []
            for y in range(8):
                at = 12 + c * 576 + i * 24 + 3 * y
                low = [w * got_low[pl.ds(at + k, 8), :] for k, w in enumerate(low_weights)]
                high = [w * got_high[pl.ds(at - 5 - k, 8), :] for k, w in enumerate(high_weights)]
                p = p_ref[pl.ds(i * 8 + y, 1), :]
                q = q_ref[pl.ds(i * 8 + y, 1), :]
                for h, slope in enumerate((low, high)):
                    here = slice(y * 16 + h * 8, y * 16 + h * 8 + 8)
                    r = before[here] - along[here] * (slope[0] + slope[1] + slope[2])
                    now.append(r)
                    carry[c * 2 + h] = carry[c * 2 + h] + p * r
                    carry[6 + c * 2 + h] = carry[6 + c * 2 + h] + q * r
            pred[c, rows, :] = jnp.concatenate(now, axis=0)
        return tuple(carry)

    sums = lax.fori_loop(0, 8, eight_rows, tuple(jnp.zeros((8, 128), f32) for _ in range(12)))
    lows = [(0.5 * step_size) * v_ref[1, 0:16, :] * below[c] for c in range(3)]
    highs = [(0.5 * step_size) * v_ref[1, 3056:3072, :] * above[c] for c in range(3)]
    copies = []
    for c in range(3):
        pred[c, 0:16] += lows[c]
        copies.append(pltpu.make_async_copy(pred.at[c, 0:1024], out.at[c, 0:1024], sems.at[c]))
        copies[c].start()
    sums = lax.fori_loop(8, 24, eight_rows, sums)
    for c in range(3):
        pred[c, 3056:3072] -= highs[c]
        for h in range(2):
            at = slice(c * 16 + h * 8, c * 16 + h * 8 + 8)
            half = slice(h * 8, h * 8 + 8)
            k = c * 2 + h
            both[0, at] = sums[k] + p_ref[0:1] * lows[c][half] - p_ref[191:192] * highs[c][half]
            both[1, at] = sums[6 + k] + q_ref[0:1] * lows[c][half] - q_ref[191:192] * highs[c][half]
    for copy in copies:
        copy.wait()


def written(start, count, pred, onto, out, token, sems):
    token[...] = jnp.zeros_like(token)
    rows = pl.ds(start, count)
    copies = [pltpu.make_async_copy(pred.at[c, rows], out.at[c, rows], sems.at[c]) for c in range(3)]
    for copy in copies:
        copy.start()
    for copy in copies:
        copy.wait()


def pairs(both, other, after, *sent):
    place = lax.axis_index("wall")
    for k, out in zip(hops, sent):
        side = jnp.where(place + k < 8, 0, 1)
        out[...] = both[side] + other[side]


def finish(pred, p_ref, q_ref, both, other, got_0, got_1, got_2, out, staged, sems):
    place = lax.axis_index("wall")
    second = place % 2 == 1
    low = jnp.where(second, other[0], 0.0)
    high = both[1] + jnp.where(second, 0.0, other[1])
    for k, got in zip(hops, (got_0, got_1, got_2)):
        value = got[...]
        low += jnp.where(place >= k, value, 0.0)
        high += jnp.where(place >= k, 0.0, value)
    carry = tuple(part[c * 16 : c * 16 + 16] for part in (low, high) for c in range(3))
    copies = []
    for part in range(6):

        def body(i, carry):
            carry = list(carry)
            for c in range(3):
                rows = pl.ds(pl.multiple_of(part * 512 + i * 128, 128), 128)
                r = pred[c, rows, :]
                now = []
                for u in range(8):
                    y = part * 32 + i * 8 + u
                    p = p_ref[pl.ds(y, 1), :]
                    q = q_ref[pl.ds(y, 1), :]
                    here = r[u * 16 : u * 16 + 16]
                    carry[c] = carry[c] + p * here
                    carry[3 + c] = carry[3 + c] - q * here
                    now.append(q * carry[c] + p * carry[3 + c])
                staged[c, rows, :] = jnp.concatenate(now, axis=0)
            return tuple(carry)

        carry = lax.fori_loop(0, 4, body, carry)
        for c in range(3):
            rows = pl.ds(part * 512, 512)
            copy = pltpu.make_async_copy(staged.at[c, rows], out.at[c, rows], sems.at[part * 3 + c])
            copy.start()
            copies.append(copy)
    for copy in copies:
        copy.wait()


def on_device(velocity, viscosity):
    groups = lax.axis_size("wall")
    spans = lax.axis_size("span")
    streams = lax.axis_size("stream")
    DMA = pltpu.SemaphoreType.DMA
    shape = jax.ShapeDtypeStruct
    block = (3, 3072, 128)

    ANY = pl.BlockSpec(memory_space=pl.ANY)
    by_row = pltpu.with_memory_space_constraint(velocity.reshape(3, 192, 16, 1, 128), pltpu.HBM)
    edge = shape((584, 3, 1, 128), f32)
    own_low, own_high = call(
        edge_rows, (edge, edge), [HBM_SPEC], (VMEM_SPEC,) * 2, [DMA((6,))], "edge_rows", (by_row,), (0, 3600000)
    )
    got_low = lax.ppermute(own_high.reshape(1752, 128), "stream", ring(streams, 1))
    got_high = lax.ppermute(own_low.reshape(1752, 128), "stream", ring(streams, -1))

    flat = velocity.reshape(block)
    layer = shape((3, 16, 128), f32)
    z_edges = call(
        stage,
        shape((576, 128), f32),
        [VMEM_SPEC, ANY],
        VMEM_SPEC,
        [],
        "stage",
        (flat, own_low),
        (9000000, 10000000),
    )
    z_next = lax.ppermute(z_edges, "span", ring(spans, -1))
    z_prev = lax.ppermute(z_edges, "span", ring(spans, 1))
    sums = shape((48, 128), f32)
    pred, y_first, y_last = call(
        interior,
        (shape(block, f32), layer, layer),
        [VMEM_SPEC, ANY],
        (VMEM_SPEC,) * 3,
        [],
        "interior",
        (flat, z_edges),
        (60000000, 10000000),
    )
    below = lax.ppermute(y_last, "wall", [(i, i + 1) for i in range(groups - 1)])
    above = lax.ppermute(y_first, "wall", [(i + 1, i) for i in range(groups - 1)])

    own_rows = shape((192, 128), f32)
    p, q = call(
        homogeneous,
        (own_rows, own_rows),
        [VMEM_SPEC, ANY],
        (VMEM_SPEC,) * 2,
        [pltpu.VMEM((16, 128), f32), pltpu.VMEM((256, 128), f32)],
        "homogeneous",
        (viscosity.reshape(12, 128), y_first),
        (3000000, 32768),
    )

    pred = call(
        patch,
        shape(block, f32),
        [VMEM_SPEC] * 4 + [ANY],
        VMEM_SPEC,
        [pltpu.VMEM((576, 128), f32)],
        "patch",
        (pred, z_edges, z_next, z_prev, p),
        (20000000, 10000000),
        {0: 0},
    )
    got_low = call(
        arrived, shape(got_low.shape, f32), [VMEM_SPEC], VMEM_SPEC, [], "arrived", (got_low,), (0, 1024), {0: 0}
    )
    pred, both, predictor = call(
        faces,
        (shape(block, f32), shape((2, 48, 128), f32), pltpu.HBM(block, f32)),
        [VMEM_SPEC] * 8,
        (VMEM_SPEC, VMEM_SPEC, HBM_SPEC),
        [DMA((3,))],
        "faces",
        (pred, flat, got_low, got_high, below, above, p, q),
        (20000000, 10000000),
        {0: 0},
    )

    other = lax.ppermute(both, "wall", [(i, i ^ 1) for i in range(groups)])

    def write(onto, start, count):
        return call(
            functools.partial(written, start, count),
            (pltpu.HBM(block, f32), shape((8, 128), f32)),
            [VMEM_SPEC, HBM_SPEC],
            (HBM_SPEC, VMEM_SPEC),
            [DMA((3,))],
            "written",
            (pred, onto),
            (0, count * 3072),
            {1: 0},
        )

    predictor, after = write(predictor, 1024, 1024)
    sent = call(
        pairs, (sums,) * 3, [VMEM_SPEC] * 2 + [ANY], (VMEM_SPEC,) * 3, [], "pairs", (both, other, after), (40000, 150000)
    )
    got = [lax.ppermute(value, "wall", ring(groups, k)) for k, value in zip(hops, sent)]
    predictor, after = write(predictor, 2048, 1024)
    velocity_new = call(
        finish,
        pltpu.HBM(block, f32),
        [VMEM_SPEC] * 8,
        HBM_SPEC,
        [pltpu.VMEM(block, f32), DMA((18,))],
        "finish",
        (pred, p, q, both, other, *got),
        (9000000, 10000000),
    )
    return predictor.reshape(velocity.shape), velocity_new.reshape(velocity.shape)


def solution(mesh):
    return jax.shard_map(
        on_device,
        mesh=mesh,
        in_specs=(P(None, "wall", "stream", "span"), P()),
        out_specs=(P(None, "wall", "stream", "span"), P(None, "wall", "stream", "span")),
        check_vma=False,
    )
```

```python
import functools

import jax
import jax.numpy as jnp
from jax import lax
from jax.experimental import pallas as pl
from jax.experimental.pallas import tpu as pltpu
from jax.sharding import PartitionSpec as P

step_size = 0.5
scale = step_size / 60.0
f32 = jnp.float32
VMEM_SPEC = pl.BlockSpec(memory_space=pltpu.VMEM)
HBM_SPEC = pl.BlockSpec(memory_space=pltpu.HBM)
LIMIT = 12 << 20
hops = (2, 4, 6)


def ring(count, shift):
    return [(i, (i + shift) % count) for i in range(count)]


def call(kernel, outs, in_specs, out_specs, scratch, name, args, cost, aliases=None):
    flops, moved = cost
    return pl.pallas_call(
        kernel,
        out_shape=outs,
        in_specs=in_specs,
        out_specs=out_specs,
        scratch_shapes=scratch,
        name=name,
        input_output_aliases=aliases or {},
        cost_estimate=pl.CostEstimate(flops=flops, bytes_accessed=moved, transcendentals=0),
        compiler_params=pltpu.CompilerParams(vmem_limit_bytes=LIMIT),
    )(*args)


def edge_rows(v_ref, low, high, sems):
    copies = []
    for c in range(3):
        to = pl.ds(4 + 192 * c, 192)
        copies.append(pltpu.make_async_copy(v_ref.at[c, :, 13:16], high.at[to], sems.at[c]))
        copies.append(pltpu.make_async_copy(v_ref.at[c, :, 0:3], low.at[to], sems.at[3 + c]))
    for copy in copies:
        copy.start()
    for ref in (low, high):
        ref[0:4] = jnp.zeros((4, 3, 1, 128), f32)
        ref[580:584] = jnp.zeros((4, 3, 1, 128), f32)
    for copy in copies:
        copy.wait()


def stage(v_ref, after, z_edges):
    lane = lax.broadcasted_iota(jnp.int32, (8, 128), 1)

    def body(step, carry):
        for u in range(4):
            t = step * 4 + u
            for c in range(3):
                pieces = []
                for i in range(16):
                    f = v_ref[c, pl.ds(pl.multiple_of(t * 128 + i * 8, 8), 8), :]
                    here = (lane >= 8 * i) & (lane < 8 * i + 8)
                    pieces.append(jnp.where(here, pltpu.roll(f, 8 * i + 3, 1), 0.0))
                while len(pieces) > 1:
                    pieces = [pieces[k] + pieces[k + 1] for k in range(0, len(pieces), 2)]
                z_edges[pl.ds(pl.multiple_of(c * 192 + t * 8, 8), 8), :] = pieces[0]
        return carry

    lax.fori_loop(0, 6, body, 0)


def shifted(value, distance, fill):
    rows, lanes = value.shape
    lane = lax.broadcasted_iota(jnp.int32, value.shape, 1)
    row = lax.broadcasted_iota(jnp.int32, value.shape, 0)
    flat = row * lanes + lane
    whole, part = divmod(abs(distance), lanes)
    if distance > 0:
        out = pltpu.roll(value, whole, 0) if whole else value
        if part:
            out = pltpu.roll(out, part, 1)
            out = jnp.where(lane < part, pltpu.roll(out, 1, 0), out)
        return jnp.where(flat < distance, fill, out)
    out = pltpu.roll(value, rows - whole, 0) if whole else value
    if part:
        out = pltpu.roll(out, lanes - part, 1)
        out = jnp.where(lane >= lanes - part, pltpu.roll(out, rows - 1, 0), out)
    return jnp.where(flat >= rows * lanes + distance, fill, out)


def homogeneous(nu_ref, after, p_ref, q_ref, table, column):
    row = lax.broadcasted_iota(jnp.int32, (16, 128), 0)
    lane = lax.broadcasted_iota(jnp.int32, (16, 128), 1)
    table[...] = jnp.ones((16, 128), f32)
    table[0:12] = nu_ref[...]
    low_face = table[...]
    high_face = shifted(low_face, -1, 1.0)
    high_face = jnp.where((row == 11) & (lane == 127), low_face, high_face)

    def products(face, towards):
        r = jnp.where(row < 12, 1.0 / face, 0.0)
        m = [1.0 + r, r, jnp.where(row < 12, 1.0, 0.0), jnp.ones((16, 128), f32)]
        k = 1
        while k < 1536:
            o = [shifted(v, towards * k, fill) for v, fill in zip(m, (1.0, 0.0, 0.0, 1.0))]
            m = [
                m[0] * o[0] + m[1] * o[2],
                m[0] * o[1] + m[1] * o[3],
                m[2] * o[0] + m[3] * o[2],
                m[2] * o[1] + m[3] * o[3],
            ]
            k *= 2
        return m, r

    before, r_low = products(low_face, 1)
    after_it, r_high = products(high_face, -1)
    p, flux = before[1], before[3]
    last = p + r_high * (flux + p)
    wronskian = jnp.broadcast_to(last[11:12, 127:128], (16, 128))
    place = lax.axis_index("wall")
    first = (place * 3) // 2
    skip = (place % 2) * 64
    sub = lax.broadcasted_iota(jnp.int32, (128, 128), 0)
    across = lax.broadcasted_iota(jnp.int32, (128, 128), 1)
    for values, out in ((p, p_ref), (after_it[1] / wronskian, q_ref)):
        table[...] = values
        for half in range(2):
            line = jnp.broadcast_to(table[pl.ds(first + half, 1), :], (128, 128))
            turned = jnp.sum(jnp.where(sub == across, line, 0.0), axis=1, keepdims=True)
            column[half * 128 : half * 128 + 128] = jnp.broadcast_to(turned, (128, 128))
        out[...] = column[pl.ds(pl.multiple_of(skip, 64), 192), :]


def interior(v_ref, after, pred, y_first, y_last):
    sub = lax.broadcasted_iota(jnp.int32, (8, 128), 0)
    source = lax.broadcasted_iota(jnp.int32, (256, 128), 0) % 128
    target = lax.broadcasted_iota(jnp.int32, (256, 128), 1)
    apart = source - target
    band = jnp.zeros((256, 128), f32)
    for m, weight in ((1, 45.0), (2, -9.0), (3, 1.0)):
        band = jnp.where(apart == m, weight, jnp.where(apart == -m, -weight, band))
    band = band.astype(jnp.bfloat16)

    def eight_rows(i, first, last):
        base = i * 128

        def part(comp, offset):
            return v_ref[comp, pl.ds(base + offset, 8), :]

        def aligned(comp, offset, count):
            at = base + offset
            return v_ref[comp, pl.ds(at if isinstance(at, int) else pl.multiple_of(at, 8), count), :]

        speeds = [
            (aligned(0, 8 * h, 8) * scale, aligned(1, 8 * h, 8) * (0.5 * step_size), aligned(2, 8 * h, 8) * scale)
            for h in range(16)
        ]
        for c in range(3):
            f = aligned(c, 0, 128)
            upper = f.astype(jnp.bfloat16)
            lower = (f - upper.astype(f32)).astype(jnp.bfloat16)
            slope_z = jnp.dot(jnp.concatenate([upper, lower], axis=1), band, preferred_element_type=f32)
            for h in range(16):
                here = f[8 * h : 8 * h + 8]
                slope_x = None
                for m, weight in ((1, 45.0), (2, -9.0), (3, 1.0)):
                    up = pltpu.roll(here, 8 - m, 0) if last and h == 15 else part(c, 8 * h + m)
                    down = pltpu.roll(here, m, 0) if first and h == 0 else part(c, 8 * h - m)
                    if h % 2:
                        up = jnp.where(sub < 8 - m, up, 0.0)
                    else:
                        down = jnp.where(sub < m, 0.0, down)
                    term = up - down
                    term = weight * term if weight != 1.0 else term
                    slope_x = term if m == 1 else slope_x + term
                if first and h < 2:
                    slope_y = aligned(c, 16 + 8 * h, 8)
                elif last and h >= 14:
                    slope_y = -aligned(c, 8 * h - 16, 8)
                else:
                    slope_y = aligned(c, 16 + 8 * h, 8) - aligned(c, 8 * h - 16, 8)
                v0, v1, v2 = speeds[h]
                advect = v0 * slope_x + v1 * slope_y + v2 * slope_z[8 * h : 8 * h + 8]
                at = base + 8 * h
                pred[c, pl.ds(at if isinstance(at, int) else pl.multiple_of(at, 8), 8), :] = here - advect

    def body(i, carry):
        eight_rows(i, False, False)
        return carry

    eight_rows(0, True, False)
    lax.fori_loop(1, 23, body, 0)
    eight_rows(23, False, True)
    for c in range(3):
        y_first[c] = v_ref[c, 0:16]
        y_last[c] = v_ref[c, 3056:3072]


def patch(pred_in, z_edges, z_next, z_prev, after, pred, change):
    lane = lax.broadcasted_iota(jnp.int32, (8, 128), 1)
    outer = (lane < 3) | (lane >= 125)
    place = lax.broadcasted_iota(jnp.int32, (192, 128), 1) & 7
    for c in range(3):
        rows = slice(c * 192, c * 192 + 192)
        n = z_next[rows]
        up = pltpu.roll(n, 125, 1)
        up -= jnp.where(place >= 1, 9.0 * pltpu.roll(n, 126, 1), 0.0)
        up += jnp.where(place >= 2, 45.0 * pltpu.roll(n, 127, 1), 0.0)
        n = z_prev[rows]
        down = jnp.where(place <= 4, 9.0 * pltpu.roll(n, 2, 1), 0.0) - pltpu.roll(n, 3, 1)
        down -= jnp.where(place <= 3, 45.0 * pltpu.roll(n, 1, 1), 0.0)
        change[rows] = jnp.where(place < 3, up, down) * (z_edges[384:576] * scale)

    def body(i, carry):
        for t in (2 * i, 2 * i + 1):
            for c in range(3):
                packed = change[pl.ds(pl.multiple_of(c * 192 + t * 8, 8), 8), :]
                rows = pl.ds(pl.multiple_of(t * 128, 128), 128)
                before = pred_in[c, rows, :]
                now = []
                for k in range(16):
                    back = jnp.where(outer, pltpu.roll(packed, 125 - 8 * k, 1), 0.0)
                    now.append(before[k * 8 : k * 8 + 8] - back)
                pred[c, rows, :] = jnp.concatenate(now, axis=0)
        return carry

    lax.fori_loop(0, 12, body, 0)


def arrived(got, out):
    pass


def faces(pred_in, v_ref, got_low, got_high, below, above, p_ref, q_ref, pred, both, out, sems):
    sub = lax.broadcasted_iota(jnp.int32, (8, 128), 0)
    low_weights = [jnp.where(sub <= 2 - k, w * scale, 0.0) for k, w in enumerate((-1.0, 9.0, -45.0))]
    high_weights = [jnp.where(sub >= 5 + k, w * scale, 0.0) for k, w in enumerate((1.0, -9.0, 45.0))]

    def eight_rows(i, carry):
        carry = list(carry)
        for c in range(3):
            rows = pl.ds(pl.multiple_of(i * 128, 128), 128)
            before = pred_in[c, rows, :]
            along = v_ref[0, rows, :]
            now = []
            for y in range(8):
                at = 12 + c * 576 + i * 24 + 3 * y
                low = [w * got_low[pl.ds(at + k, 8), :] for k, w in enumerate(low_weights)]
                high = [w * got_high[pl.ds(at - 5 - k, 8), :] for k, w in enumerate(high_weights)]
                p = p_ref[pl.ds(i * 8 + y, 1), :]
                q = q_ref[pl.ds(i * 8 + y, 1), :]
                for h, slope in enumerate((low, high)):
                    here = slice(y * 16 + h * 8, y * 16 + h * 8 + 8)
                    r = before[here] - along[here] * (slope[0] + slope[1] + slope[2])
                    now.append(r)
                    carry[c * 2 + h] = carry[c * 2 + h] + p * r
                    carry[6 + c * 2 + h] = carry[6 + c * 2 + h] + q * r
            pred[c, rows, :] = jnp.concatenate(now, axis=0)
        return tuple(carry)

    sums = lax.fori_loop(0, 8, eight_rows, tuple(jnp.zeros((8, 128), f32) for _ in range(12)))
    lows = [(0.5 * step_size) * v_ref[1, 0:16, :] * below[c] for c in range(3)]
    highs = [(0.5 * step_size) * v_ref[1, 3056:3072, :] * above[c] for c in range(3)]
    copies = []
    for c in range(3):
        pred[c, 0:16] += lows[c]
        copies.append(pltpu.make_async_copy(pred.at[c, 0:1024], out.at[c, 0:1024], sems.at[c]))
        copies[c].start()
    sums = lax.fori_loop(8, 24, eight_rows, sums)
    for c in range(3):
        pred[c, 3056:3072] -= highs[c]
        for h in range(2):
            at = slice(c * 16 + h * 8, c * 16 + h * 8 + 8)
            half = slice(h * 8, h * 8 + 8)
            k = c * 2 + h
            both[0, at] = sums[k] + p_ref[0:1] * lows[c][half] - p_ref[191:192] * highs[c][half]
            both[1, at] = sums[6 + k] + q_ref[0:1] * lows[c][half] - q_ref[191:192] * highs[c][half]
    for copy in copies:
        copy.wait()


def written(start, count, pred, onto, out, token, sems):
    token[...] = jnp.zeros_like(token)
    rows = pl.ds(start, count)
    copies = [pltpu.make_async_copy(pred.at[c, rows], out.at[c, rows], sems.at[c]) for c in range(3)]
    for copy in copies:
        copy.start()
    for copy in copies:
        copy.wait()


def pairs(both, other, after, *sent):
    place = lax.axis_index("wall")
    for k, out in zip(hops, sent):
        side = jnp.where(place + k < 8, 0, 1)
        out[...] = both[side] + other[side]


def finish(pred, p_ref, q_ref, both, other, got_0, got_1, got_2, out, staged, sems):
    place = lax.axis_index("wall")
    second = place % 2 == 1
    low = jnp.where(second, other[0], 0.0)
    high = both[1] + jnp.where(second, 0.0, other[1])
    for k, got in zip(hops, (got_0, got_1, got_2)):
        value = got[...]
        low += jnp.where(place >= k, value, 0.0)
        high += jnp.where(place >= k, 0.0, value)
    carry = tuple(part[c * 16 : c * 16 + 16] for part in (low, high) for c in range(3))
    copies = []
    for part in range(6):

        def body(i, carry):
            carry = list(carry)
            for c in range(3):
                rows = pl.ds(pl.multiple_of(part * 512 + i * 128, 128), 128)
                r = pred[c, rows, :]
                now = []
                for u in range(8):
                    y = part * 32 + i * 8 + u
                    p = p_ref[pl.ds(y, 1), :]
                    q = q_ref[pl.ds(y, 1), :]
                    here = r[u * 16 : u * 16 + 16]
                    carry[c] = carry[c] + p * here
                    carry[3 + c] = carry[3 + c] - q * here
                    now.append(q * carry[c] + p * carry[3 + c])
                staged[c, rows, :] = jnp.concatenate(now, axis=0)
            return tuple(carry)

        carry = lax.fori_loop(0, 4, body, carry)
        for c in range(3):
            rows = pl.ds(part * 512, 512)
            copy = pltpu.make_async_copy(staged.at[c, rows], out.at[c, rows], sems.at[part * 3 + c])
            copy.start()
            copies.append(copy)
    for copy in copies:
        copy.wait()


def on_device(velocity, viscosity):
    groups = lax.axis_size("wall")
    spans = lax.axis_size("span")
    streams = lax.axis_size("stream")
    DMA = pltpu.SemaphoreType.DMA
    shape = jax.ShapeDtypeStruct
    block = (3, 3072, 128)

    ANY = pl.BlockSpec(memory_space=pl.ANY)
    by_row = pltpu.with_memory_space_constraint(velocity.reshape(3, 192, 16, 1, 128), pltpu.HBM)
    edge = shape((584, 3, 1, 128), f32)
    own_low, own_high = call(
        edge_rows, (edge, edge), [HBM_SPEC], (VMEM_SPEC,) * 2, [DMA((6,))], "edge_rows", (by_row,), (0, 3600000)
    )
    got_low = lax.ppermute(own_high.reshape(1752, 128), "stream", ring(streams, 1))
    got_high = lax.ppermute(own_low.reshape(1752, 128), "stream", ring(streams, -1))

    flat = velocity.reshape(block)
    layer = shape((3, 16, 128), f32)
    z_edges = call(
        stage,
        shape((576, 128), f32),
        [VMEM_SPEC, ANY],
        VMEM_SPEC,
        [],
        "stage",
        (flat, own_low),
        (9000000, 10000000),
    )
    z_next = lax.ppermute(z_edges, "span", ring(spans, -1))
    z_prev = lax.ppermute(z_edges, "span", ring(spans, 1))
    sums = shape((48, 128), f32)
    pred, y_first, y_last = call(
        interior,
        (shape(block, f32), layer, layer),
        [VMEM_SPEC, ANY],
        (VMEM_SPEC,) * 3,
        [],
        "interior",
        (flat, z_edges),
        (60000000, 10000000),
    )
    below = lax.ppermute(y_last, "wall", [(i, i + 1) for i in range(groups - 1)])
    above = lax.ppermute(y_first, "wall", [(i + 1, i) for i in range(groups - 1)])

    own_rows = shape((192, 128), f32)
    p, q = call(
        homogeneous,
        (own_rows, own_rows),
        [VMEM_SPEC, ANY],
        (VMEM_SPEC,) * 2,
        [pltpu.VMEM((16, 128), f32), pltpu.VMEM((256, 128), f32)],
        "homogeneous",
        (viscosity.reshape(12, 128), y_first),
        (3000000, 32768),
    )

    pred = call(
        patch,
        shape(block, f32),
        [VMEM_SPEC] * 4 + [ANY],
        VMEM_SPEC,
        [pltpu.VMEM((576, 128), f32)],
        "patch",
        (pred, z_edges, z_next, z_prev, p),
        (20000000, 10000000),
        {0: 0},
    )
    got_low = call(
        arrived, shape(got_low.shape, f32), [VMEM_SPEC], VMEM_SPEC, [], "arrived", (got_low,), (0, 1024), {0: 0}
    )
    pred, both, predictor = call(
        faces,
        (shape(block, f32), shape((2, 48, 128), f32), pltpu.HBM(block, f32)),
        [VMEM_SPEC] * 8,
        (VMEM_SPEC, VMEM_SPEC, HBM_SPEC),
        [DMA((3,))],
        "faces",
        (pred, flat, got_low, got_high, below, above, p, q),
        (20000000, 10000000),
        {0: 0},
    )

    other = lax.ppermute(both, "wall", [(i, i ^ 1) for i in range(groups)])

    def write(onto, start, count):
        return call(
            functools.partial(written, start, count),
            (pltpu.HBM(block, f32), shape((8, 128), f32)),
            [VMEM_SPEC, HBM_SPEC],
            (HBM_SPEC, VMEM_SPEC),
            [DMA((3,))],
            "written",
            (pred, onto),
            (0, count * 3072),
            {1: 0},
        )

    predictor, after = write(predictor, 1024, 1024)
    sent = call(
        pairs, (sums,) * 3, [VMEM_SPEC] * 2 + [ANY], (VMEM_SPEC,) * 3, [], "pairs", (both, other, after), (40000, 150000)
    )
    got = [lax.ppermute(value, "wall", ring(groups, k)) for k, value in zip(hops, sent)]
    predictor, after = write(predictor, 2048, 1024)
    velocity_new = call(
        finish,
        pltpu.HBM(block, f32),
        [VMEM_SPEC] * 8,
        HBM_SPEC,
        [pltpu.VMEM(block, f32), DMA((18,))],
        "finish",
        (pred, p, q, both, other, *got),
        (9000000, 10000000),
    )
    return predictor.reshape(velocity.shape), velocity_new.reshape(velocity.shape)


def solution(mesh):
    return jax.shard_map(
        on_device,
        mesh=mesh,
        in_specs=(P(None, "wall", "stream", "span"), P()),
        out_specs=(P(None, "wall", "stream", "span"), P(None, "wall", "stream", "span")),
        check_vma=False,
    )
```
